32 devices in a mesh: req: 16 (over z, x, core), exp: 2 (over y).
Axes of the slice: x: 2, y: 2, z: 4, core: 2. Of those that a mesh axis runs over, the one named last changes fastest.
Arguments:
- residual: bfloat16 [32, 64, 2560], P(('exp', 'req')), may hold values from -40 to 40
- queries: bfloat16 [32, 64, 2560], P(('exp', 'req')), may hold values from -95 to 95
- fresh_kv: bfloat16 [32, 64, 1024], P(('exp', 'req')), may hold values from -5.1 to 5.1
- cache_key_value: bfloat16 [2048, 32, 1024], P('req', 'exp'), may hold values from -5 to 5
- lengths: int32 [32], P(('exp', 'req')), may hold values from 256 to 2048, as said below
- expert_ids: int32 [32, 64, 6], P(('exp', 'req')), may hold values from 0 to 15, all different within a row; in each aligned block of 64 rows (0 to 63, 64 to 127, ..., all dimensions but the last counted through in order) at most 30 rows name the same one
- router_w: float32 [32, 64, 6], P(('exp', 'req')), may hold values from 0.2 to 1
- norm_gain: float32 [2560], replicated, may hold values from 0.5 to 1.5
- gate_w: bfloat16 [16, 2560, 1536], P('req', None, 'exp'), may hold values from -0.125 to 0.125
- up_w: bfloat16 [16, 2560, 1536], P('req', None, 'exp'), may hold values from -0.125 to 0.125
- down_w: bfloat16 [16, 2560, 1536], P('req', None, 'exp'), may hold values from -0.15625 to 0.15625
Outputs:
- mixed: bfloat16 [32, 64, 2560], P(('exp', 'req'))
The draws below stay inside these ranges and needn't reach their ends.
Inputs may be any that keep to these rules, and one draw needn't show every extreme that they name: `expert_ids`: each token names 6 different experts. Among the tokens of one request no expert is named more than 30 times, and in every draw some expert is named exactly 30 times by one request. `lengths`: some request has exactly 2048 cached positions.
All inputs are finite; a program needn't handle non-finite values.
Results may differ from the reference program's by a relative error of at most 0.006.
Values may be sent and summed in bfloat16 or wider, within the bound.
A program may use at most 128 MiB of HBM per device.

```python
import math
import jax
import jax.numpy as jnp
import numpy as np
from jax import lax

D = 2560
QUERY_HEADS = 20
KEY_VALUE_HEADS = 4
HEAD_SIZE = 128
FF = 1536
TOP = 6
NEW_TOKENS = 64
CACHE_SLOTS = 2048
EXPERTS = 16
FBLK = 768
REQUEST_COUNT = 32
CAP = 30
N_EXP = 2


def key_start(key):
    sampled_draws = jax.random.normal(jax.random.fold_in(key, 11), (REQUEST_COUNT, NEW_TOKENS, 2 * KEY_VALUE_HEADS * HEAD_SIZE), jnp.float32)
    return jnp.clip(sampled_draws, -5.0, 5.0)


def draw_fresh_kv(key, part):
    base_offset = key_start(key)
    return base_offset.astype(jnp.bfloat16)


def draw_queries(key, part):
    drawn = jnp.clip(jax.random.normal(jax.random.fold_in(key, 13), (REQUEST_COUNT, NEW_TOKENS, QUERY_HEADS * HEAD_SIZE), jnp.float32), -5.0, 5.0)
    return drawn.astype(jnp.bfloat16)


def draw_residual(key, part):
    shape = (REQUEST_COUNT, NEW_TOKENS, D)
    base_offset = jnp.clip(jax.random.normal(jax.random.fold_in(key, 21), shape, jnp.float32), -4.0, 4.0)
    lower, upper = (0.3, 3.0)
    row_scale = jnp.exp(jax.random.uniform(jax.random.fold_in(key, 22), (REQUEST_COUNT, NEW_TOKENS, 1), jnp.float32, math.log(lower), math.log(upper)))
    col_scale = jnp.exp(jax.random.uniform(jax.random.fold_in(key, 23), (1, 1, D), jnp.float32, math.log(lower), math.log(upper)))
    return (base_offset * row_scale * col_scale).astype(jnp.bfloat16)


def draw_lengths(key, part):
    sampled_draws = jax.random.randint(jax.random.fold_in(key, 31), (REQUEST_COUNT,), CACHE_SLOTS // 8, CACHE_SLOTS + 1)
    longest = jax.random.randint(jax.random.fold_in(key, 32), (), 0, REQUEST_COUNT)
    return jnp.where(jnp.arange(REQUEST_COUNT) == longest, CACHE_SLOTS, sampled_draws).astype(jnp.int32)


def block_levels(key, extent, pieces, low, largest):
    loudness, own = 1.0, jax.random.fold_in(key, 6)
    for axis_at, parts in pieces:
        heights = jnp.exp(jax.random.uniform(jax.random.fold_in(own, axis_at), (parts,), jnp.float32, low / len(pieces), largest / len(pieces)))
        loudness = loudness * jnp.repeat(heights, extent[axis_at] // parts).reshape([-1 if axis == axis_at else 1 for axis in range(len(extent))])
    return loudness


def shared_out(own_key, own, number, rows, count, top, bound, lean):
    ranking = jax.random.permutation(own_key, count)
    crowded, ordinary = shares(count, rows * top, bound, lean, True), shares(count, rows * top, bound, lean, False)
    places = jnp.arange(count)

    def named(sizes, turn):
        used = int((sizes > 0).sum())
        fixed = max(1, used // 4)
        moved = fixed + (places - fixed + turn * (used - fixed)) % max(1, count - fixed)
        return jnp.zeros((count,), jnp.int32).at[ranking[jnp.where(places < fixed, places, moved)]].set(jnp.asarray(sizes, jnp.int32))

    sizes = jnp.where(number % 4 == 0, named(crowded, number // 4), named(ordinary, number - number // 4 - 1))
    mixed = jax.random.permutation(jax.random.fold_in(own, 3), count)
    donor, sink = mixed[0:count // 2 * 2:2], mixed[1:count // 2 * 2:2]
    margin = jnp.minimum(sizes[donor] - 1, bound - sizes[sink]) // 2
    margin = jnp.where((donor == ranking[0]) | (sink == ranking[0]) | (sizes[sink] == 0), 0, jnp.maximum(margin, 0))
    moved = jax.random.randint(jax.random.fold_in(own, 4), (count // 2,), 0, 1 << 20) % (margin + 1)
    sizes = sizes.at[donor].add(-moved).at[sink].add(moved)
    items = jnp.searchsorted(jnp.cumsum(sizes), jnp.arange(rows * top), side="right").astype(jnp.int32)
    listing = items.reshape(top, rows).T
    listing = listing[jax.random.permutation(jax.random.fold_in(own, 1), rows)]
    turn = jax.random.randint(jax.random.fold_in(own, 2), (rows, 1), 0, top)
    return jnp.take_along_axis(listing, (jnp.arange(top)[None, :] + turn) % top, axis=1)


def shares(amount, total, most, skew, full):
    loads = [(1 << 20) // math.isqrt(standing ** skew) + 1 for standing in range(1, amount + 1)]
    largest = most if full else min(most, max(-(-total // amount), total * loads[0] // sum(loads)))
    least = 1 if total - largest >= amount - 1 else 0
    given, rest = [largest] + [least] * (amount - 1), total - largest - least * (amount - 1)
    while rest > 0:
        movable = [i for i in range(1, amount) if given[i] < largest] or [i for i in range(1, amount) if given[i] < most]
        mass, left = sum([loads[i] for i in movable]), rest
        for i in movable:
            extra = min(most - given[i], max(1, left * loads[i] // mass), rest)
            given[i] = given[i] + extra
            rest = rest - extra
    return np.array(given)


def centred(stream_key, shape, spread, reach, split=(), kind=jnp.bfloat16):
    array = spread * jax.random.normal(stream_key, shape, jnp.float32)
    if split:
        array = array * block_levels(stream_key, shape, split, -0.22, 0.18)
    return jnp.clip(array, -reach, reach).astype(kind)


def setup_inputs(seed: int = 0) -> dict:
    key_of = jax.random.split(jax.random.key(seed), 12)
    residual = draw_residual(jax.random.fold_in(key_of[11], 71), 0)
    queries = draw_queries(jax.random.fold_in(key_of[11], 71), 0)
    fresh_kv = draw_fresh_kv(jax.random.fold_in(key_of[11], 71), 0)
    cache_key_value = centred(key_of[3], (CACHE_SLOTS, REQUEST_COUNT, 2 * KEY_VALUE_HEADS * HEAD_SIZE), 1.0, 5.0, ((0, 16), (1, 2)))
    lengths = draw_lengths(jax.random.fold_in(key_of[11], 71), 0)
    expert_ids_keys = jax.random.split(jax.random.fold_in(key_of[5], 1), REQUEST_COUNT * NEW_TOKENS // NEW_TOKENS)
    expert_ids_turns = jax.random.permutation(jax.random.fold_in(key_of[5], 3), REQUEST_COUNT * NEW_TOKENS // NEW_TOKENS)
    expert_ids = jax.vmap(lambda own, number: shared_out(jax.random.fold_in(key_of[5], 2), own, number, NEW_TOKENS, EXPERTS, TOP, CAP, 1))(expert_ids_keys, expert_ids_turns).reshape((REQUEST_COUNT, NEW_TOKENS, TOP))
    router_w = jnp.clip(0.2 + 0.8 * jax.random.uniform(key_of[6], (REQUEST_COUNT, NEW_TOKENS, TOP), jnp.float32) ** block_levels(key_of[6], (REQUEST_COUNT, NEW_TOKENS, TOP), ((0, 32),), -0.2, 0.2), 0.2, 1.0)
    norm_gain = jnp.clip(1.0 + 0.1 * jax.random.normal(key_of[7], (D,), jnp.float32), 0.5, 1.5)
    gate_w = centred(key_of[8], (EXPERTS, D, FF), D ** -0.5, 0.125, ((0, 16), (2, 2)))
    up_w = centred(key_of[9], (EXPERTS, D, FF), D ** -0.5, 0.125, ((0, 16), (2, 2)))
    down_w = centred(key_of[10], (EXPERTS, D, FF), FF ** -0.5, 0.15625, ((0, 16), (2, 2)))
    return dict(residual=residual, queries=queries, fresh_kv=fresh_kv, cache_key_value=cache_key_value, lengths=lengths, expert_ids=expert_ids, router_w=router_w, norm_gain=norm_gain, gate_w=gate_w, up_w=up_w, down_w=down_w)


def attend_request(query_matrix, cached_entries, recent_entries, length):
    group_size = QUERY_HEADS // KEY_VALUE_HEADS
    key_value_keys = KEY_VALUE_HEADS * HEAD_SIZE
    joined_rows = jnp.concatenate([cached_entries, recent_entries], axis=0).astype(jnp.float32)
    joined_keys = joined_rows[:, :key_value_keys].reshape(-1, KEY_VALUE_HEADS, HEAD_SIZE)
    joined_values = joined_rows[:, key_value_keys:].reshape(-1, KEY_VALUE_HEADS, HEAD_SIZE)
    grouped_queries = query_matrix.astype(jnp.float32).reshape(NEW_TOKENS, KEY_VALUE_HEADS, group_size, HEAD_SIZE)
    scores = jnp.einsum('tgjd,sgd->gjts', grouped_queries, joined_keys) / math.sqrt(HEAD_SIZE)
    place = jnp.arange(CACHE_SLOTS + NEW_TOKENS)[None, :]
    token_pos = jnp.arange(NEW_TOKENS)[:, None]
    visible = jnp.where(place < CACHE_SLOTS, place < length, place - CACHE_SLOTS <= token_pos)
    scores = jnp.where(visible, scores, -jnp.inf)
    peak = lax.optimization_barrier(jnp.max(scores, axis=-1, keepdims=True))
    raised = jnp.exp(scores - peak)
    probs = (raised / lax.optimization_barrier(jnp.sum(raised, axis=-1, keepdims=True))).astype(jnp.bfloat16)
    summed = jnp.einsum('gjts,sgd->tgjd', probs.astype(jnp.float32), joined_values)
    return summed.reshape(NEW_TOKENS, QUERY_HEADS * HEAD_SIZE).astype(jnp.bfloat16)

def slot_table(ids):
    flat_ids = ids.reshape(-1).astype(jnp.int32)
    one_hot = (flat_ids[:, None] == jnp.arange(EXPERTS, dtype=jnp.int32)[None, :]).astype(jnp.int32)
    slot_of = lax.optimization_barrier(jnp.sum((jnp.cumsum(one_hot, axis=0) - 1) * one_hot, axis=1)).astype(jnp.int32)
    return (flat_ids, slot_of)

def reference(residual, queries, fresh_kv, cache_key_value, lengths, expert_ids, router_w, norm_gain, gate_w, up_w, down_w):

    def attend_one(index):
        cached_entries = lax.dynamic_index_in_dim(cache_key_value, index, axis=1, keepdims=False)
        return attend_request(queries[index], cached_entries, fresh_kv[index], lengths[index])
    attended = lax.map(attend_one, jnp.arange(REQUEST_COUNT, dtype=jnp.int32))
    hidden = residual.astype(jnp.float32) + attended.astype(jnp.float32)
    normed = (hidden * lax.rsqrt(lax.optimization_barrier(jnp.mean(hidden * hidden, axis=-1, keepdims=True)) + 1e-06) * norm_gain).astype(jnp.bfloat16)
    flat_ids, slot_of = jax.vmap(slot_table)(expert_ids)

    def fill(normed_rows, ids_row, slots_row):
        empty = jnp.zeros((EXPERTS, CAP, D), jnp.bfloat16)
        return empty.at[ids_row, slots_row].set(jnp.repeat(normed_rows, TOP, axis=0))
    buffers = jax.vmap(fill)(normed, flat_ids, slot_of)

    def run_expert(expert):
        rows = lax.dynamic_index_in_dim(buffers, expert, axis=1, keepdims=False).reshape(REQUEST_COUNT * CAP, D)
        gate_val = jnp.dot(rows, gate_w[expert], preferred_element_type=jnp.float32)
        up_val = jnp.dot(rows, up_w[expert], preferred_element_type=jnp.float32)
        active = (jax.nn.silu(gate_val) * up_val).astype(jnp.bfloat16)
        active_blocks = active.astype(jnp.float32).reshape(REQUEST_COUNT * CAP, N_EXP, FBLK)
        down_blocks = down_w[expert].astype(jnp.float32).reshape(D, N_EXP, FBLK)
        partial_value = jnp.einsum('rkf,dkf->krd', active_blocks, down_blocks).astype(jnp.bfloat16)
        result = lax.optimization_barrier(jnp.sum(partial_value.astype(jnp.float32), axis=0))
        return result.astype(jnp.bfloat16).reshape(REQUEST_COUNT, CAP, D)
    produced = lax.map(run_expert, jnp.arange(EXPERTS, dtype=jnp.int32))

    def combine_one(index):
        picked = produced[flat_ids[index], index, slot_of[index]].astype(jnp.float32).reshape(NEW_TOKENS, TOP, D)
        routed = lax.optimization_barrier(jnp.sum(router_w[index][:, :, None] * picked, axis=1))
        return (hidden[index] + routed).astype(jnp.bfloat16)
    return lax.map(combine_one, jnp.arange(REQUEST_COUNT, dtype=jnp.int32))
```

```python
import math

import jax
import jax.numpy as jnp
from jax import lax
from jax.sharding import PartitionSpec as P

QUERY_HEADS = 20
KEY_VALUE_HEADS = 4
HEAD_SIZE = 128


def block_terms(batch_rows, gate_blocks, up_blocks, down_blocks):
    gate_val = jnp.einsum(
        "rd,kdf->krf", batch_rows, gate_blocks, preferred_element_type=jnp.float32
    )
    up_val = jnp.einsum("rd,kdf->krf", batch_rows, up_blocks, preferred_element_type=jnp.float32)
    active = (jax.nn.silu(gate_val) * up_val).astype(jnp.bfloat16)
    partial_value = jnp.einsum(
        "krf,kdf->krd", active, down_blocks, preferred_element_type=jnp.float32
    ).astype(jnp.bfloat16)
    return jnp.sum(partial_value.astype(jnp.float32), axis=0)


def per_device(
    residual,
    queries,
    fresh_kv,
    cache_key_value,
    lengths,
    expert_ids,
    router_w,
    norm_gain,
    gate_w,
    up_w,
    down_w,
):
    pages = lax.all_to_all(cache_key_value, "req", split_axis=1, concat_axis=0, tiled=True)
    token_count = residual.shape[1]
    width = residual.shape[2]
    group_size = QUERY_HEADS // KEY_VALUE_HEADS
    key_value_keys = KEY_VALUE_HEADS * HEAD_SIZE
    grouped_queries = queries[0].reshape(token_count, KEY_VALUE_HEADS, group_size, HEAD_SIZE)
    cached_entries = pages[:, 0, :]
    recent_entries = fresh_kv[0]
    stored_keys = cached_entries[:, :key_value_keys].reshape(-1, KEY_VALUE_HEADS, HEAD_SIZE)
    stored_values = cached_entries[:, key_value_keys:].reshape(-1, KEY_VALUE_HEADS, HEAD_SIZE)
    recent_keys = recent_entries[:, :key_value_keys].reshape(-1, KEY_VALUE_HEADS, HEAD_SIZE)
    recent_values = recent_entries[:, key_value_keys:].reshape(-1, KEY_VALUE_HEADS, HEAD_SIZE)
    scale = 1.0 / math.sqrt(HEAD_SIZE)
    score_old = (
        jnp.einsum(
            "tgjd,pgd->gjtp", grouped_queries, stored_keys, preferred_element_type=jnp.float32
        )
        * scale
    )
    score_new = (
        jnp.einsum(
            "tgjd,cgd->gjtc", grouped_queries, recent_keys, preferred_element_type=jnp.float32
        )
        * scale
    )
    length = lengths[0]
    score_old = jnp.where(jnp.arange(cached_entries.shape[0]) < length, score_old, -jnp.inf)
    token_pos = jnp.arange(token_count)
    score_new = jnp.where(token_pos[None, :] <= token_pos[:, None], score_new, -jnp.inf)
    peak = jnp.maximum(jnp.max(score_old, axis=-1), jnp.max(score_new, axis=-1))[..., None]
    raised_old = jnp.exp(score_old - peak)
    raised_new = jnp.exp(score_new - peak)
    summed = jnp.sum(raised_old, axis=-1, keepdims=True) + jnp.sum(
        raised_new, axis=-1, keepdims=True
    )
    probs_old = (raised_old / summed).astype(jnp.bfloat16)
    probs_new = (raised_new / summed).astype(jnp.bfloat16)
    attended = jnp.einsum(
        "gjtp,pgd->tgjd", probs_old, stored_values, preferred_element_type=jnp.float32
    )
    attended = attended + jnp.einsum(
        "gjtc,cgd->tgjd", probs_new, recent_values, preferred_element_type=jnp.float32
    )
    attended = attended.reshape(token_count, width).astype(jnp.bfloat16)
    hidden = residual[0].astype(jnp.float32) + attended.astype(jnp.float32)
    normed = (
        hidden * lax.rsqrt(jnp.mean(hidden * hidden, axis=-1, keepdims=True) + 1e-06) * norm_gain
    ).astype(jnp.bfloat16)
    experts = lax.axis_size("req") * gate_w.shape[0]
    top_k = expert_ids.shape[2]
    capacity = min(token_count, 5 * token_count * top_k // (4 * experts))
    chosen = expert_ids[0][:, :, None] == jnp.arange(experts, dtype=jnp.int32)
    named = jnp.any(chosen, axis=1)
    weight = jnp.sum(jnp.where(chosen, router_w[0][:, :, None], 0.0), axis=1)
    place = jnp.cumsum(named.astype(jnp.int32), axis=0) - 1
    slots = jnp.arange(capacity, dtype=jnp.int32)
    held = named[:, :, None] & (place[:, :, None] == slots)
    held = held.reshape(token_count, experts * capacity)
    outbound = jnp.einsum(
        "ts,td->sd", held.astype(jnp.bfloat16), normed, preferred_element_type=jnp.float32
    )
    outbound = outbound.astype(jnp.bfloat16).reshape(experts, capacity, width)
    inbound = lax.all_to_all(outbound, "req", split_axis=0, concat_axis=0, tiled=True)
    batch_rows = inbound.reshape(-1, width)
    produced = block_terms(
        batch_rows,
        lax.all_gather(gate_w[0], "exp", axis=0),
        lax.all_gather(up_w[0], "exp", axis=0),
        lax.all_gather(down_w[0], "exp", axis=0),
    )
    produced = produced.astype(jnp.bfloat16).reshape(inbound.shape)
    returned = lax.all_to_all(produced, "req", split_axis=0, concat_axis=0, tiled=True)
    returned = returned.reshape(experts * capacity, width)
    scaled = jnp.where(held, jnp.repeat(weight, capacity, axis=1), 0.0)
    upper = lax.reduce_precision(scaled, 8, 7)
    lower = (scaled - upper).astype(jnp.bfloat16)
    routed = jnp.dot(
        upper.astype(jnp.bfloat16), returned, preferred_element_type=jnp.float32
    ) + jnp.dot(lower, returned, preferred_element_type=jnp.float32)
    mixed = (hidden + routed).astype(jnp.bfloat16)
    return mixed[None]


def solution(mesh):
    in_specs = (
        P(("exp", "req"), None, None),
        P(("exp", "req"), None, None),
        P(("exp", "req"), None, None),
        P("req", "exp", None),
        P(("exp", "req")),
        P(("exp", "req"), None, None),
        P(("exp", "req"), None, None),
        P(),
        P("req", None, "exp"),
        P("req", None, "exp"),
        P("req", None, "exp"),
    )
    out_specs = P(("exp", "req"), None, None)
    return jax.shard_map(
        per_device, mesh=mesh, in_specs=in_specs, out_specs=out_specs, check_vma=False
    )
```

```python
import math

import jax
import jax.numpy as jnp
from jax import lax
from jax.sharding import PartitionSpec as P

QUERY_HEADS = 20
KEY_VALUE_HEADS = 4
HEAD_SIZE = 128
PARTS = 2


def hidden_units(batch_rows, gate_blocks, up_blocks):
    gate_val = jnp.einsum(
        "rd,kdf->krf", batch_rows, gate_blocks, preferred_element_type=jnp.float32
    )
    up_val = jnp.einsum("rd,kdf->krf", batch_rows, up_blocks, preferred_element_type=jnp.float32)
    return (jax.nn.silu(gate_val) * up_val).astype(jnp.bfloat16)


def block_term(active, down_part):
    return jnp.einsum(
        "rf,df->rd", active, down_part, preferred_element_type=jnp.float32
    ).astype(jnp.bfloat16)


def per_device(
    residual,
    queries,
    fresh_kv,
    cache_key_value,
    lengths,
    expert_ids,
    router_w,
    norm_gain,
    gate_w,
    up_w,
    down_w,
):
    pages = lax.all_to_all(cache_key_value, "req", split_axis=1, concat_axis=0, tiled=True)
    token_count = residual.shape[1]
    width = residual.shape[2]
    group_size = QUERY_HEADS // KEY_VALUE_HEADS
    key_value_keys = KEY_VALUE_HEADS * HEAD_SIZE
    grouped_queries = queries[0].reshape(token_count, KEY_VALUE_HEADS, group_size, HEAD_SIZE)
    cached_entries = pages[:, 0, :]
    recent_entries = fresh_kv[0]
    stored_keys = cached_entries[:, :key_value_keys].reshape(-1, KEY_VALUE_HEADS, HEAD_SIZE)
    stored_values = cached_entries[:, key_value_keys:].reshape(-1, KEY_VALUE_HEADS, HEAD_SIZE)
    recent_keys = recent_entries[:, :key_value_keys].reshape(-1, KEY_VALUE_HEADS, HEAD_SIZE)
    recent_values = recent_entries[:, key_value_keys:].reshape(-1, KEY_VALUE_HEADS, HEAD_SIZE)
    scale = 1.0 / math.sqrt(HEAD_SIZE)
    score_old = (
        jnp.einsum(
            "tgjd,pgd->gjtp", grouped_queries, stored_keys, preferred_element_type=jnp.float32
        )
        * scale
    )
    score_new = (
        jnp.einsum(
            "tgjd,cgd->gjtc", grouped_queries, recent_keys, preferred_element_type=jnp.float32
        )
        * scale
    )
    length = lengths[0]
    score_old = jnp.where(jnp.arange(cached_entries.shape[0]) < length, score_old, -jnp.inf)
    token_pos = jnp.arange(token_count)
    score_new = jnp.where(token_pos[None, :] <= token_pos[:, None], score_new, -jnp.inf)
    peak = jnp.maximum(jnp.max(score_old, axis=-1), jnp.max(score_new, axis=-1))[..., None]
    raised_old = jnp.exp(score_old - peak)
    raised_new = jnp.exp(score_new - peak)
    summed = jnp.sum(raised_old, axis=-1, keepdims=True) + jnp.sum(
        raised_new, axis=-1, keepdims=True
    )
    probs_old = (raised_old / summed).astype(jnp.bfloat16)
    probs_new = (raised_new / summed).astype(jnp.bfloat16)
    attended = jnp.einsum(
        "gjtp,pgd->tgjd", probs_old, stored_values, preferred_element_type=jnp.float32
    )
    attended = attended + jnp.einsum(
        "gjtc,cgd->tgjd", probs_new, recent_values, preferred_element_type=jnp.float32
    )
    attended = attended.reshape(token_count, width).astype(jnp.bfloat16)
    hidden = residual[0].astype(jnp.float32) + attended.astype(jnp.float32)
    normed = (
        hidden * lax.rsqrt(jnp.mean(hidden * hidden, axis=-1, keepdims=True) + 1e-06) * norm_gain
    ).astype(jnp.bfloat16)
    experts = lax.axis_size("req") * gate_w.shape[0]
    top_k = expert_ids.shape[2]
    capacity = min(token_count, 5 * token_count * top_k // (4 * experts))
    capacity = -(-capacity // 8) * 8
    chosen = expert_ids[0][:, :, None] == jnp.arange(experts, dtype=jnp.int32)
    named = jnp.any(chosen, axis=1)
    weight = jnp.sum(jnp.where(chosen, router_w[0][:, :, None], 0.0), axis=1)
    place = jnp.cumsum(named.astype(jnp.int32), axis=0) - 1
    slots = jnp.arange(capacity, dtype=jnp.int32)
    held = named[:, :, None] & (place[:, :, None] == slots)
    held = held.reshape(token_count, experts * capacity)
    outbound = jnp.einsum(
        "ts,td->sd", held.astype(jnp.bfloat16), normed, preferred_element_type=jnp.float32
    )
    outbound = outbound.astype(jnp.bfloat16).reshape(experts, capacity, width)
    inbound = lax.all_to_all(outbound, "req", split_axis=0, concat_axis=0, tiled=True)
    batch_rows = inbound.reshape(-1, width)
    active = hidden_units(
        batch_rows, lax.all_gather(gate_w[0], "exp", axis=0), lax.all_gather(up_w[0], "exp", axis=0)
    )
    sharers = lax.axis_size("exp")
    place_in_exp = lax.axis_index("exp")
    own = lax.dynamic_index_in_dim(active, place_in_exp, 0, keepdims=False)
    guests = []
    for shift in range(1, sharers):
        other = lax.rem(place_in_exp + shift, sharers)
        sent = lax.dynamic_index_in_dim(active, other, 0, keepdims=False)
        there = [(i, (i + shift) % sharers) for i in range(sharers)]
        guests.append(lax.ppermute(sent, "exp", there))
    scaled = jnp.where(held, jnp.repeat(weight, capacity, axis=1), 0.0)
    upper = lax.reduce_precision(scaled, 8, 7)
    lower = (scaled - upper).astype(jnp.bfloat16)
    upper = upper.astype(jnp.bfloat16)
    part = width // PARTS
    last = None
    routed = []
    for piece in range(PARTS):
        down_part = down_w[0, piece * part : (piece + 1) * part]
        total = block_term(own, down_part).astype(jnp.float32)
        for shift in range(1, sharers):
            term = block_term(guests[shift - 1], down_part)
            if last is not None:
                term, last = lax.optimization_barrier((term, last))
            back = [(i, (i - shift) % sharers) for i in range(sharers)]
            last = lax.ppermute(term, "exp", back)
            total = total + last.astype(jnp.float32)
        produced = total.astype(jnp.bfloat16).reshape(experts, capacity, part)
        returned = lax.all_to_all(produced, "req", split_axis=0, concat_axis=0, tiled=True)
        returned = returned.reshape(experts * capacity, part)
        routed.append(
            jnp.dot(upper, returned, preferred_element_type=jnp.float32)
            + jnp.dot(lower, returned, preferred_element_type=jnp.float32)
        )
    routed = jnp.concatenate(routed, axis=1)
    mixed = (hidden + routed).astype(jnp.bfloat16)
    return mixed[None]


def solution(mesh):
    in_specs = (
        P(("exp", "req"), None, None),
        P(("exp", "req"), None, None),
        P(("exp", "req"), None, None),
        P("req", "exp", None),
        P(("exp", "req")),
        P(("exp", "req"), None, None),
        P(("exp", "req"), None, None),
        P(),
        P("req", None, "exp"),
        P("req", None, "exp"),
        P("req", None, "exp"),
    )
    out_specs = P(("exp", "req"), None, None)
    return jax.shard_map(
        per_device, mesh=mesh, in_specs=in_specs, out_specs=out_specs, check_vma=False
    )
```
